32 devices in a mesh: rows: 8 (over z, y), chan: 4 (over x, core).
Axes of the slice: x: 2, y: 2, z: 4, core: 2. Of those that a mesh axis runs over, the one named last changes fastest.
Arguments:
- latent: bfloat16 [32, 128, 1280], P('rows', None, 'chan'), may hold values from -6 to 6
- stale_latent: bfloat16 [16, 128, 1280], P('rows', None, 'chan'), may hold values from -6 to 6
- stale_hidden: bfloat16 [16, 128, 1280], P('rows', None, 'chan'), may hold values from -4 to 4
- first_kernel: bfloat16 [3, 3, 1280, 1280], P(None, None, None, 'chan'), may hold values from -0.0546875 to 0.0546875
- second_kernel: bfloat16 [3, 3, 1280, 1280], P(None, None, None, 'chan'), may hold values from -0.0546875 to 0.0546875
- scale_table: float32 [1000, 1280], P(None, 'chan'), may hold values from 0.3 to 3
- timestep: int32 [1], replicated, may hold values from 0 to 999
- cotangent: bfloat16 [32, 128, 1280], P('rows', None, 'chan'), may hold values from -6 to 6
Outputs:
- output: bfloat16 [32, 128, 1280], P('rows', None, 'chan')
- grad_latent: bfloat16 [32, 128, 1280], P('rows', None, 'chan')
- grad_first: float32 [3, 3, 1280, 1280], P(None, None, 'rows', 'chan')
- grad_second: float32 [3, 3, 1280, 1280], P(None, None, 'rows', 'chan')
The draws below stay inside these ranges and needn't reach their ends.
Inputs may be any that keep to these rules, and one draw needn't show every extreme that they name: `timestep`: selects a row of scale_table.
All inputs are finite; a program needn't handle non-finite values.
Results may differ from the reference program's by a relative error of at most 0.0058.
Values may be sent and summed in bfloat16 or wider, within the bound.
A program may use at most 192 MiB of HBM per device.

```python
import math
import jax
import jax.numpy as jnp
from jax import lax

C = 1280
W = 128
ROWS_DEV = 4
STEPS = 1000
H = 32
N_ROWS = 8


def strengthened(entries, key, source, target, parts, factor):
    owner, partner = [(jnp.arange(entries.shape[dim]) // (entries.shape[dim] // parts)).reshape([-1 if axis == dim else 1 for axis in range(entries.ndim)]) for dim in (source, target)]
    chosen = jax.random.permutation(key, parts)[partner]
    strong = (owner == chosen) | (owner == (partner + parts // 2) % parts)
    return jnp.where(strong, factor * entries, entries)


def block_levels(rng, extent, split, least, largest):
    def one(axis_at, parts):
        draws = jax.random.uniform(jax.random.fold_in(jax.random.fold_in(rng, 6), axis_at), (parts,), jnp.float32, least / len(split), largest / len(split))
        return jnp.repeat(jnp.exp(draws), extent[axis_at] // parts).reshape((-1,) + (1,) * (len(extent) - axis_at - 1))

    loudness = one(*split[0])
    for cut in split[1:]:
        loudness = loudness * one(*cut)
    return loudness


def bell_draw(stream_key, extent, scale, limit, shards=(), kind=jnp.bfloat16):
    values = jax.random.normal(stream_key, extent, jnp.float32) * scale
    if len(shards) > 0:
        values = block_levels(stream_key, extent, shards, -0.22, 0.18) * values
    return jnp.clip(values, min=-limit, max=limit).astype(kind)


def heavy_noise(stream_key, extent, scale, bound, split, heavy, dtype=jnp.bfloat16):
    entries = scale * jax.random.normal(stream_key, extent, jnp.float32)
    if split:
        entries = entries * block_levels(stream_key, extent, split, -0.22, 0.18)
    return jnp.clip(strengthened(entries, jax.random.fold_in(stream_key, 3), *heavy), -bound, bound).astype(dtype)


def setup_inputs(seed: int = 0) -> dict:
    key_list = jax.random.split(jax.random.key(seed), 9)
    latent = heavy_noise(key_list[0], (H, W, C), 1.0, 6.0, ((0, 8), (2, 4)), (0, 2, 8, 2.0))
    stale_latent = bell_draw(key_list[1], (2 * N_ROWS, W, C), 1.0, 6.0, ((0, 8), (2, 4)))
    stale_hidden = bell_draw(key_list[2], (2 * N_ROWS, W, C), 0.6, 4.0, ((0, 8), (2, 4)))
    first_kernel = bell_draw(key_list[3], (3, 3, C, C), (9 * C) ** -0.5, 0.0546875, ((3, 4),))
    second_kernel = bell_draw(key_list[4], (3, 3, C, C), (9 * C) ** -0.5, 0.0546875, ((3, 4),))
    scale_table = jnp.clip(jnp.exp(math.log(3.0) - 2.3025851 * jax.random.uniform(key_list[5], (STEPS, C), jnp.float32) ** block_levels(key_list[5], (STEPS, C), ((1, 4),), -0.2, 0.2)), 0.3, 3.0)
    timestep = jax.random.randint(key_list[6], (1,), 0, STEPS).astype(jnp.int32)
    cotangent = bell_draw(key_list[7], (H, W, C), 1.0, 6.0, ((0, 8), (2, 4)))
    return dict(latent=latent, stale_latent=stale_latent, stale_hidden=stale_hidden, first_kernel=first_kernel, second_kernel=second_kernel, scale_table=scale_table, timestep=timestep, cotangent=cotangent)


def silu_slope(values):
    logistic = jax.nn.sigmoid(values)
    return logistic * (1.0 + values * (1.0 - logistic))


def conv_rows(padded, kernel):
    result = lax.conv_general_dilated(padded[None].astype(jnp.float32), kernel.astype(jnp.float32), (1, 1), ((0, 0), (1, 1)), dimension_numbers=("NHWC", "HWIO", "NHWC"), precision=lax.Precision.HIGHEST)
    return result[0]


def flipped(kernel):
    return jnp.transpose(kernel[::-1, ::-1], (0, 1, 3, 2))


def stale_blocks(field, edges):
    block_rows = field.reshape(N_ROWS, ROWS_DEV, W, C)
    edge_rows = edges.reshape(N_ROWS, 2, W, C)
    position = jnp.arange(N_ROWS)[:, None, None]
    above = jnp.where(position > 0, edge_rows[:, 0], jnp.zeros_like(edge_rows[:, 0]))
    below = jnp.where(position < N_ROWS - 1, edge_rows[:, 1], jnp.zeros_like(edge_rows[:, 1]))
    return jnp.concatenate([above[:, None], block_rows, below[:, None]], axis=1)


def tap_sums(padded, grads):
    row_count, col_count, out_width = grads.shape
    flat_grads = grads.reshape(row_count * col_count, out_width).astype(jnp.float32)
    pieces = []
    for row_tap in range(3):
        for col_tap in range(3):
            window = padded[row_tap:row_tap + row_count, col_tap:col_tap + col_count]
            window = window.reshape(row_count * col_count, -1).astype(jnp.float32)
            pieces.append(lax.dot_general(window, flat_grads, (((0,), (0,)), ((), ())), precision=lax.Precision.HIGHEST))
    stacked = jnp.stack(pieces)
    return stacked.reshape(3, 3, stacked.shape[1], out_width)


def reference(latent, stale_latent, stale_hidden, first_kernel, second_kernel, scale_table, timestep, cotangent):
    latent_f = latent.astype(jnp.float32)
    act = jax.nn.silu(latent_f).astype(jnp.bfloat16)
    edge_act = jax.nn.silu(stale_latent.astype(jnp.float32)).astype(jnp.bfloat16)
    pre_act = lax.map(lambda padded: conv_rows(padded, first_kernel), stale_blocks(act, edge_act)).reshape(H, W, C)
    step_scale = jnp.sum(jnp.where(jnp.arange(STEPS)[:, None] == timestep[0], scale_table, 0.0), axis=0)
    scaled = pre_act * step_scale
    hidden = jax.nn.silu(scaled).astype(jnp.bfloat16)
    second = lax.map(lambda padded: conv_rows(padded, second_kernel), stale_blocks(hidden, stale_hidden)).reshape(H, W, C)
    output = (latent_f + second).astype(jnp.bfloat16)
    row_pad = ((1, 1), (0, 0), (0, 0))
    grad_hidden = conv_rows(jnp.pad(cotangent, row_pad), flipped(second_kernel))
    delta = (grad_hidden * silu_slope(scaled) * step_scale).astype(jnp.bfloat16)
    grad_pre = conv_rows(jnp.pad(delta, row_pad), flipped(first_kernel))
    grad_latent = (latent_f * 0.0 + cotangent.astype(jnp.float32) + grad_pre * silu_slope(latent_f)).astype(jnp.bfloat16)
    border = ((1, 1), (1, 1), (0, 0))
    grad_second = tap_sums(jnp.pad(hidden, border), cotangent) / H
    grad_first = tap_sums(jnp.pad(act, border), delta) / H
    return output, grad_latent, grad_first, grad_second
```

```python
import jax
import jax.numpy as jnp
from jax import lax
from jax.sharding import PartitionSpec as P


def extended(shard, sides, width):
    for axis, dim in sides:
        peers, length = (lax.axis_size(axis), shard.shape[dim])
        up = [(i, (i + 1) % peers) for i in range(peers - 1)]
        down = [(j, i) for i, j in up]
        last = lax.slice_in_dim(shard, length - width, length, axis=dim)
        leading = lax.slice_in_dim(shard, 0, width, axis=dim)
        before = lax.ppermute(last, axis, up)
        after = lax.ppermute(leading, axis, down)
        shard = jnp.concatenate([before, shard, after], axis=dim)
    return shard


def silu_slope(values):
    logistic = jax.nn.sigmoid(values)
    return logistic * (1.0 + values * (1.0 - logistic))


def conv_rows(padded, kernel):
    result = lax.conv_general_dilated(
        padded[None],
        kernel,
        (1, 1),
        ((0, 0), (1, 1)),
        dimension_numbers=("NHWC", "HWIO", "NHWC"),
        preferred_element_type=jnp.float32,
    )
    return result[0]


def flipped(kernel):
    return jnp.transpose(kernel[::-1, ::-1], (0, 1, 3, 2))


def tap_sums(field, grads):
    rows, cols, wide = field.shape
    depth = grads.shape[-1]
    padded = jnp.pad(field, ((1, 1), (1, 1), (0, 0)))
    shifted = [padded[:, tap : tap + cols].reshape((rows + 2) * cols, wide) for tap in range(3)]
    shifted = jnp.concatenate(shifted, axis=1)
    flat_grads = grads.reshape(rows * cols, depth)
    pieces = [
        lax.dot_general(
            shifted[tap * cols : tap * cols + rows * cols],
            flat_grads,
            (((0,), (0,)), ((), ())),
            preferred_element_type=jnp.float32,
        )
        for tap in range(3)
    ]
    return jnp.stack(pieces).reshape(3, 3, wide, depth)


def scatter_sum(partial, axis):
    peers = lax.axis_size(axis)
    index = lax.axis_index(axis)
    width = partial.shape[-1] // peers
    sent = partial.astype(jnp.bfloat16)
    total = lax.dynamic_slice_in_dim(partial, index * width, width, axis=2)
    for step in range(1, peers):
        block = lax.dynamic_slice_in_dim(sent, (index + step) % peers * width, width, axis=2)
        moved = lax.ppermute(block, axis, [(i, (i + step) % peers) for i in range(peers)])
        total = total + moved.astype(jnp.float32)
    return total


def own_channels(field, axis):
    peers = lax.axis_size(axis)
    rows, cols, depth = field.shape
    blocks = field.reshape(rows, cols, peers, depth // peers)
    blocks = jnp.transpose(blocks, (2, 0, 1, 3))
    moved = lax.all_to_all(blocks, axis, 0, 0, tiled=True)
    return moved.reshape(peers * rows, cols, depth // peers)


def on_device(
    latent,
    stale_latent,
    stale_hidden,
    first_kernel,
    second_kernel,
    scale_table,
    timestep,
    cotangent,
):
    row_index = lax.axis_index("rows")
    row_devices = lax.axis_size("rows")
    height = latent.shape[0] * row_devices
    inside = latent.shape[0] + 1
    latent_f = latent.astype(jnp.float32)
    act = jax.nn.silu(latent_f).astype(jnp.bfloat16)
    edge_act = jax.nn.silu(stale_latent.astype(jnp.float32)).astype(jnp.bfloat16)

    def stale_pad(field, edges):
        above = jnp.where(row_index > 0, edges[0], jnp.zeros_like(edges[0]))
        below = jnp.where(row_index < row_devices - 1, edges[1], jnp.zeros_like(edges[1]))
        return jnp.concatenate([above[None], field, below[None]], axis=0)

    grad_pad = extended(cotangent, (("rows", 0),), 1)
    act_all = lax.all_gather(stale_pad(act, edge_act), "chan", axis=2, tiled=True)
    cotangent_all = lax.all_gather(cotangent, "rows", axis=0, tiled=True)
    grad_hidden = scatter_sum(conv_rows(grad_pad, flipped(second_kernel)), "chan")
    pre_act = conv_rows(act_all, first_kernel)
    step_scale = lax.dynamic_index_in_dim(scale_table, timestep[0], 0, keepdims=False)
    scaled = pre_act * step_scale
    hidden = jax.nn.silu(scaled).astype(jnp.bfloat16)
    delta = (grad_hidden * silu_slope(scaled) * step_scale).astype(jnp.bfloat16)
    hidden_all = lax.all_gather(stale_pad(hidden, stale_hidden), "chan", axis=2, tiled=True)
    delta_pad = extended(delta, (("rows", 0),), 1)
    delta_all = lax.all_gather(delta, "rows", axis=0, tiled=True)
    act_own = own_channels(act_all[1:inside], "rows")
    output = (latent_f + conv_rows(hidden_all, second_kernel)).astype(jnp.bfloat16)
    grad_pre = scatter_sum(conv_rows(delta_pad, flipped(first_kernel)), "chan")
    grad_latent = (
        latent_f * 0.0 + cotangent.astype(jnp.float32) + grad_pre * silu_slope(latent_f)
    ).astype(jnp.bfloat16)
    hidden_own = own_channels(hidden_all[1:inside], "rows")
    grad_second = tap_sums(hidden_own, cotangent_all) / height
    grad_first = tap_sums(act_own, delta_all) / height
    return (output, grad_latent, grad_first, grad_second)


def solution(mesh):
    in_specs = (
        P("rows", None, "chan"),
        P("rows", None, "chan"),
        P("rows", None, "chan"),
        P(None, None, None, "chan"),
        P(None, None, None, "chan"),
        P(None, "chan"),
        P(),
        P("rows", None, "chan"),
    )
    out_specs = (
        P("rows", None, "chan"),
        P("rows", None, "chan"),
        P(None, None, "rows", "chan"),
        P(None, None, "rows", "chan"),
    )
    return jax.shard_map(
        on_device, mesh=mesh, in_specs=in_specs, out_specs=out_specs, check_vma=False
    )
```

```python
import functools
import jax
import jax.numpy as jnp
from jax import lax
from jax.experimental import pallas as pl
from jax.experimental.pallas import tpu as pltpu
from jax.sharding import PartitionSpec as P

VMEM_BYTES = 48 * 1024 * 1024
PARAMS = pltpu.CompilerParams(vmem_limit_bytes=VMEM_BYTES)


def silu_slope(values):
    logistic = jax.nn.sigmoid(values)
    return logistic * (1.0 + values * (1.0 - logistic))


def moved_columns(values, offset):
    if offset == 0:
        return values
    cols = values.shape[1]
    lane = lax.broadcasted_iota(jnp.int32, values.shape, 1)
    turned = pltpu.roll(values.astype(jnp.float32), (-offset) % cols, 1)
    inside = (lane + offset >= 0) & (lane + offset < cols)
    return jnp.where(inside, turned, 0.0).astype(jnp.bfloat16)


def forward_body(finish, x_ref, k_ref, *refs):
    *others, shifted, total = refs
    step = pl.program_id(0)
    rows, _, cols = x_ref.shape
    inner = rows - 2
    for col_tap in range(3):

        @pl.when(step == 3 * col_tap)
        def _():
            for row in range(rows):
                shifted[:, row * cols : (row + 1) * cols] = moved_columns(x_ref[row], col_tap - 1)

    start = pl.multiple_of(lax.rem(step, 3) * cols, cols)
    product = jnp.dot(
        k_ref[0, 0],
        shifted[:, pl.ds(start, inner * cols)],
        preferred_element_type=jnp.float32,
    )

    @pl.when(step == 0)
    def _():
        total[...] = product

    @pl.when(step > 0)
    def _():
        total[...] += product

    @pl.when(step == 8)
    def _():
        for row in range(inner):
            finish(row, total[:, row * cols : (row + 1) * cols], *others)


def forward_conv(finish, x, kernel, extras, out_shape):
    rows, depth, cols = x.shape
    wide = kernel.shape[2]
    whole = lambda array: pl.BlockSpec(array.shape, lambda t, n=len(array.shape): (0,) * n)
    flops = 2 * 9 * wide * depth * (rows - 2) * cols
    return pl.pallas_call(
        functools.partial(forward_body, finish),
        grid=(9,),
        in_specs=[
            whole(x),
            pl.BlockSpec((1, 1, wide, depth), lambda t: (t % 3, t // 3, 0, 0)),
            *[whole(extra) for extra in extras],
        ],
        out_specs=[whole(out) for out in out_shape],
        out_shape=out_shape,
        scratch_shapes=[
            pltpu.VMEM((depth, rows * cols), jnp.bfloat16),
            pltpu.VMEM((wide, (rows - 2) * cols), jnp.float32),
        ],
        compiler_params=PARAMS,
        cost_estimate=pl.CostEstimate(
            flops=flops, bytes_accessed=2 * (kernel.size + x.size), transcendentals=0
        ),
    )(x, kernel, *extras)


def finish_hidden(row, values, edge_ref, scale_ref, hidden_ref, slope_ref):
    scale = scale_ref[...]
    scaled = values * scale
    logistic = jax.nn.sigmoid(scaled)
    hidden_ref[row + 1] = (scaled * logistic).astype(jnp.bfloat16)
    slope_ref[row] = logistic * (1.0 + scaled * (1.0 - logistic)) * scale
    if row == 0:
        hidden_ref[0] = edge_ref[0]
        hidden_ref[hidden_ref.shape[0] - 1] = edge_ref[1]


def finish_output(row, values, latent_ref, out_ref):
    out_ref[row] = (latent_ref[row].astype(jnp.float32) + values).astype(jnp.bfloat16)


def backward_body(x_ref, k_ref, out_ref, shifted, total):
    step = pl.program_id(0)
    rows, depth, cols = x_ref.shape
    inner = rows - 2

    @pl.when(step == 0)
    def _():
        for col_tap in range(3):
            for row in range(rows):
                shifted[
                    col_tap * depth : (col_tap + 1) * depth, row * cols : (row + 1) * cols
                ] = moved_columns(x_ref[row], 1 - col_tap)

    start = pl.multiple_of((2 - step) * cols, cols)
    product = lax.dot_general(
        k_ref[0].reshape(3 * depth, k_ref.shape[3]),
        shifted[:, pl.ds(start, inner * cols)],
        (((0,), (0,)), ((), ())),
        preferred_element_type=jnp.float32,
    )

    @pl.when(step == 0)
    def _():
        total[...] = product

    @pl.when(step > 0)
    def _():
        total[...] += product

    @pl.when(step == 2)
    def _():
        peers, width = out_ref.shape[0], out_ref.shape[2]
        for peer in range(peers):
            for row in range(inner):
                out_ref[peer, row] = total[
                    peer * width : (peer + 1) * width, row * cols : (row + 1) * cols
                ].astype(jnp.bfloat16)


def backward_conv(x, kernel, peers):
    rows, depth, cols = x.shape
    wide = kernel.shape[3]
    out_shape = jax.ShapeDtypeStruct((peers, rows - 2, wide // peers, cols), jnp.bfloat16)
    return pl.pallas_call(
        backward_body,
        grid=(3,),
        in_specs=[
            pl.BlockSpec(x.shape, lambda t: (0, 0, 0)),
            pl.BlockSpec((1, 3, depth, wide), lambda t: (t, 0, 0, 0)),
        ],
        out_specs=pl.BlockSpec(out_shape.shape, lambda t: (0, 0, 0, 0)),
        out_shape=out_shape,
        scratch_shapes=[
            pltpu.VMEM((3 * depth, rows * cols), jnp.bfloat16),
            pltpu.VMEM((wide, (rows - 2) * cols), jnp.float32),
        ],
        compiler_params=PARAMS,
        cost_estimate=pl.CostEstimate(
            flops=2 * 9 * wide * depth * (rows - 2) * cols,
            bytes_accessed=2 * (kernel.size + x.size),
            transcendentals=0,
        ),
    )(x, kernel)


def weights_body(scale, starts_ref, field_ref, *refs):
    *grads, out_ref, shifted, total = refs
    shares, blocks, share, wide, cols = field_ref.shape
    rows, depth, _ = grads[0].shape
    height = blocks * rows
    edge = jnp.zeros((wide, cols), jnp.bfloat16)
    for tap in range(3):
        shifted[tap, :, 0:cols] = edge
        shifted[tap, :, (height + 1) * cols : (height + 2) * cols] = edge
    for place in range(rows):

        def shift_block(block, carry, place=place):
            piece = field_ref[place // share, block, place % share]
            span = pl.ds(pl.multiple_of((block * rows + place + 1) * cols, cols), cols)
            for tap in range(3):
                shifted[tap, :, span] = moved_columns(piece, tap - 1)
            return carry

        lax.fori_loop(0, blocks, shift_block, 0)
    for at, grad_ref in enumerate(grads):
        flat = jnp.concatenate([grad_ref[row] for row in range(rows)], axis=1)
        for row_tap in range(3):
            span = pl.ds(pl.multiple_of((starts_ref[at] + row_tap) * cols, cols), rows * cols)
            if wide % 16 == 0:
                product = lax.dot_general(
                    shifted[:, :, span].reshape(3 * wide, rows * cols),
                    flat,
                    (((1,), (1,)), ((), ())),
                    preferred_element_type=jnp.float32,
                ).reshape(3, wide, depth)
                total[row_tap] = product if at == 0 else total[row_tap] + product
            else:
                for tap in range(3):
                    product = lax.dot_general(
                        shifted[tap, :, span],
                        flat,
                        (((1,), (1,)), ((), ())),
                        preferred_element_type=jnp.float32,
                    )
                    total[row_tap, tap] = product if at == 0 else total[row_tap, tap] + product
    out_ref[...] = total[...] * scale


def weight_grads(starts, field, grads):
    shares, blocks, share, wide, cols = field.shape
    rows, depth, _ = grads[0].shape
    height = blocks * rows
    out_shape = jax.ShapeDtypeStruct((3, 3, wide, depth), jnp.float32)
    vmem = pl.BlockSpec(memory_space=pltpu.VMEM)
    return pl.pallas_call(
        functools.partial(weights_body, 1.0 / height),
        in_specs=[pl.BlockSpec(memory_space=pltpu.SMEM), vmem, *[vmem for _ in grads]],
        out_specs=vmem,
        out_shape=out_shape,
        scratch_shapes=[
            pltpu.VMEM((3, wide, (height + 2) * cols), jnp.bfloat16),
            pltpu.VMEM(out_shape.shape, jnp.float32),
        ],
        compiler_params=PARAMS,
        cost_estimate=pl.CostEstimate(
            flops=2 * 9 * wide * depth * height * cols,
            bytes_accessed=2 * field.size + 2 * len(grads) * grads[0].size + 4 * 9 * wide * depth,
            transcendentals=0,
        ),
    )(starts, field, *grads)


def cycle_order(peers):
    return list(range(0, peers, 2)) + list(range(1, peers, 2))[::-1]


def ring_blocks(block, axis):
    peers = lax.axis_size(axis)
    order = cycle_order(peers)
    ahead = [(order[i], order[(i + 1) % peers]) for i in range(peers)]
    back = [(j, i) for i, j in ahead]
    blocks = [block]
    left = right = block
    for hop in range(1, peers // 2 + 1):
        left = lax.ppermute(left, axis, ahead)
        blocks.append(left)
        if hop <= (peers - 1) // 2:
            right = lax.ppermute(right, axis, back)
            blocks.append(right)
    return blocks


def ring_starts(axis, rows):
    peers = lax.axis_size(axis)
    order = cycle_order(peers)
    place = [order.index(i) for i in range(peers)]
    at = jnp.asarray(place, jnp.int32)[lax.axis_index(axis)]
    offsets = [0]
    for hop in range(1, peers // 2 + 1):
        offsets.append(-hop)
        if hop <= (peers - 1) // 2:
            offsets.append(hop)
    where = (at + jnp.asarray(offsets, jnp.int32)) % peers
    return jnp.asarray(order, jnp.int32)[where] * rows


def with_rims(shard, axis):
    peers = lax.axis_size(axis)
    up = [(i, i + 1) for i in range(peers - 1)]
    down = [(j, i) for i, j in up]
    before = lax.ppermute(shard[-1:], axis, up)
    after = lax.ppermute(shard[:1], axis, down)
    return jnp.concatenate([before, shard, after], axis=0)


def scatter_sum(blocks, axis):
    peers = lax.axis_size(axis)
    index = lax.axis_index(axis)
    total = lax.dynamic_index_in_dim(blocks, index, 0, keepdims=False).astype(jnp.float32)
    for step in range(1, peers):
        block = lax.dynamic_index_in_dim(blocks, (index + step) % peers, 0, keepdims=False)
        moved = lax.ppermute(block, axis, [(i, (i + step) % peers) for i in range(peers)])
        total = total + moved.astype(jnp.float32)
    return total


def own_channels(field, axis, others):
    peers = lax.axis_size(axis)
    shares = lax.axis_size(others)
    rows, depth, cols = field.shape
    share = rows // shares
    part = lax.dynamic_slice_in_dim(field, lax.axis_index(others) * share, share, axis=0)
    part = part.reshape(share, peers, depth // peers, cols)
    part = jnp.transpose(part, (1, 0, 2, 3))
    part = lax.all_to_all(part, axis, 0, 0, tiled=True)
    return lax.all_gather(part, others, axis=0)


def on_device(
    latent,
    stale_latent,
    stale_hidden,
    first_kernel,
    second_kernel,
    scale_table,
    timestep,
    cotangent,
):
    row_index = lax.axis_index("rows")
    row_devices = lax.axis_size("rows")
    peers = lax.axis_size("chan")
    upright = lambda field: jnp.transpose(field, (0, 2, 1))
    latent, stale_latent, stale_hidden, cotangent = [
        upright(field) for field in (latent, stale_latent, stale_hidden, cotangent)
    ]
    first = jnp.transpose(first_kernel, (0, 1, 3, 2))
    second = jnp.transpose(second_kernel, (0, 1, 3, 2))
    rows, depth, cols = latent.shape
    latent_f = latent.astype(jnp.float32)
    act = jax.nn.silu(latent_f).astype(jnp.bfloat16)
    edge_act = jax.nn.silu(stale_latent.astype(jnp.float32)).astype(jnp.bfloat16)
    present = jnp.stack([row_index > 0, row_index < row_devices - 1])[:, None, None]
    edge_act = jnp.where(present, edge_act, jnp.zeros_like(edge_act))
    edge_hidden = jnp.where(present, stale_hidden, jnp.zeros_like(stale_hidden))
    act_pad = jnp.concatenate([edge_act[:1], act, edge_act[1:]], axis=0)
    act_all = lax.all_gather(act_pad, "chan", axis=1, tiled=True)
    step_scale = lax.dynamic_index_in_dim(scale_table, timestep[0], 0, keepdims=False)
    scale_map = jnp.broadcast_to(step_scale[:, None], (depth, cols))
    starts = ring_starts("rows", rows)

    grad_hidden = scatter_sum(backward_conv(with_rims(cotangent, "rows"), second, peers), "chan")
    hidden_pad, slope = forward_conv(
        finish_hidden,
        act_all,
        first,
        (edge_hidden, scale_map),
        [
            jax.ShapeDtypeStruct((rows + 2, depth, cols), jnp.bfloat16),
            jax.ShapeDtypeStruct((rows, depth, cols), jnp.float32),
        ],
    )
    hidden_all = lax.all_gather(hidden_pad, "chan", axis=1, tiled=True)
    delta = (grad_hidden * slope).astype(jnp.bfloat16)
    grad_pre = scatter_sum(backward_conv(with_rims(delta, "rows"), first, peers), "chan")
    grad_latent = (
        latent_f * 0.0 + cotangent.astype(jnp.float32) + grad_pre * silu_slope(latent_f)
    ).astype(jnp.bfloat16)
    (output,) = forward_conv(
        finish_output,
        hidden_all,
        second,
        (latent,),
        [jax.ShapeDtypeStruct((rows, depth, cols), jnp.bfloat16)],
    )
    act_own = own_channels(act_all[1:-1], "rows", "chan")
    hidden_own = own_channels(hidden_all[1:-1], "rows", "chan")
    grad_first = weight_grads(starts, act_own, ring_blocks(delta, "rows"))
    grad_second = weight_grads(starts, hidden_own, ring_blocks(cotangent, "rows"))
    return (upright(output), upright(grad_latent), grad_first, grad_second)


def solution(mesh):
    in_specs = (
        P("rows", None, "chan"),
        P("rows", None, "chan"),
        P("rows", None, "chan"),
        P(None, None, None, "chan"),
        P(None, None, None, "chan"),
        P(None, "chan"),
        P(),
        P("rows", None, "chan"),
    )
    out_specs = (
        P("rows", None, "chan"),
        P("rows", None, "chan"),
        P(None, None, "rows", "chan"),
        P(None, None, "rows", "chan"),
    )
    return jax.shard_map(
        on_device, mesh=mesh, in_specs=in_specs, out_specs=out_specs, check_vma=False
    )
```

```python
import functools
import jax
import jax.numpy as jnp
from jax import lax
from jax.experimental import pallas as pl
from jax.experimental.pallas import tpu as pltpu
from jax.sharding import PartitionSpec as P

VMEM_BYTES = 48 * 1024 * 1024
PARAMS = pltpu.CompilerParams(vmem_limit_bytes=VMEM_BYTES)


def silu_slope(values):
    logistic = jax.nn.sigmoid(values)
    return logistic * (1.0 + values * (1.0 - logistic))


def moved_columns(values, offset):
    if offset == 0:
        return values
    cols = values.shape[1]
    lane = lax.broadcasted_iota(jnp.int32, values.shape, 1)
    turned = pltpu.roll(values.astype(jnp.float32), (-offset) % cols, 1)
    inside = (lane + offset >= 0) & (lane + offset < cols)
    return jnp.where(inside, turned, 0.0).astype(jnp.bfloat16)


def shifted_sums(values, offset):
    cols = values.shape[1]
    lane = lax.broadcasted_iota(jnp.int32, values.shape, 1)
    inside = (lane + offset >= 0) & (lane + offset < cols)
    return jnp.where(inside, pltpu.roll(values, (-offset) % cols, 1), 0.0)


def forward_body(finish, x_ref, k_ref, *refs):
    *others, flat, total = refs
    step = pl.program_id(0)
    rows, _, cols = x_ref.shape
    inner = rows - 2
    wide = k_ref.shape[2]

    @pl.when(step == 0)
    def _():
        for row in range(rows):
            flat[:, row * cols : (row + 1) * cols] = x_ref[row]

    start = pl.multiple_of(step * cols, cols)
    product = jnp.dot(
        k_ref[0].reshape(3 * wide, k_ref.shape[3]),
        flat[:, pl.ds(start, inner * cols)],
        preferred_element_type=jnp.float32,
    )

    @pl.when(step == 0)
    def _():
        total[...] = product

    @pl.when(step > 0)
    def _():
        total[...] += product

    @pl.when(step == 2)
    def _():
        for row in range(inner):
            left, middle, right = [
                total[tap * wide : (tap + 1) * wide, row * cols : (row + 1) * cols]
                for tap in range(3)
            ]
            sums = middle + shifted_sums(left, -1) + shifted_sums(right, 1)
            finish(row, sums, *others)


def forward_conv(finish, x, kernel, extras, out_shape):
    rows, depth, cols = x.shape
    wide = kernel.shape[2]
    whole = lambda array: pl.BlockSpec(array.shape, lambda t, n=len(array.shape): (0,) * n)
    flops = 2 * 9 * wide * depth * (rows - 2) * cols
    return pl.pallas_call(
        functools.partial(forward_body, finish),
        grid=(3,),
        in_specs=[
            whole(x),
            pl.BlockSpec((1, 3, wide, depth), lambda t: (t, 0, 0, 0)),
            *[whole(extra) for extra in extras],
        ],
        out_specs=[whole(out) for out in out_shape],
        out_shape=out_shape,
        scratch_shapes=[
            pltpu.VMEM((depth, rows * cols), jnp.bfloat16),
            pltpu.VMEM((3 * wide, (rows - 2) * cols), jnp.float32),
        ],
        compiler_params=PARAMS,
        cost_estimate=pl.CostEstimate(
            flops=flops, bytes_accessed=2 * (kernel.size + x.size), transcendentals=0
        ),
    )(x, kernel, *extras)


def finish_hidden(row, values, edge_ref, scale_ref, hidden_ref, slope_ref):
    scale = scale_ref[...]
    scaled = values * scale
    logistic = jax.nn.sigmoid(scaled)
    hidden_ref[row + 1] = (scaled * logistic).astype(jnp.bfloat16)
    slope_ref[row] = logistic * (1.0 + scaled * (1.0 - logistic)) * scale
    if row == 0:
        hidden_ref[0] = edge_ref[0]
        hidden_ref[hidden_ref.shape[0] - 1] = edge_ref[1]


def finish_output(row, values, latent_ref, out_ref):
    out_ref[row] = (latent_ref[row].astype(jnp.float32) + values).astype(jnp.bfloat16)


def backward_body(x_ref, k_ref, out_ref, shifted, total):
    step = pl.program_id(0)
    rows, depth, cols = x_ref.shape
    inner = rows - 2

    @pl.when(step == 0)
    def _():
        for col_tap in range(3):
            for row in range(rows):
                shifted[
                    col_tap * depth : (col_tap + 1) * depth, row * cols : (row + 1) * cols
                ] = moved_columns(x_ref[row], 1 - col_tap)

    start = pl.multiple_of((2 - step) * cols, cols)
    product = lax.dot_general(
        k_ref[0].reshape(3 * depth, k_ref.shape[3]),
        shifted[:, pl.ds(start, inner * cols)],
        (((0,), (0,)), ((), ())),
        preferred_element_type=jnp.float32,
    )

    @pl.when(step == 0)
    def _():
        total[...] = product

    @pl.when(step > 0)
    def _():
        total[...] += product

    @pl.when(step == 2)
    def _():
        peers, width = out_ref.shape[0], out_ref.shape[2]
        for peer in range(peers):
            for row in range(inner):
                out_ref[peer, row] = total[
                    peer * width : (peer + 1) * width, row * cols : (row + 1) * cols
                ].astype(jnp.bfloat16)


def backward_conv(x, kernel, peers):
    rows, depth, cols = x.shape
    wide = kernel.shape[3]
    out_shape = jax.ShapeDtypeStruct((peers, rows - 2, wide // peers, cols), jnp.bfloat16)
    return pl.pallas_call(
        backward_body,
        grid=(3,),
        in_specs=[
            pl.BlockSpec(x.shape, lambda t: (0, 0, 0)),
            pl.BlockSpec((1, 3, depth, wide), lambda t: (t, 0, 0, 0)),
        ],
        out_specs=pl.BlockSpec(out_shape.shape, lambda t: (0, 0, 0, 0)),
        out_shape=out_shape,
        scratch_shapes=[
            pltpu.VMEM((3 * depth, rows * cols), jnp.bfloat16),
            pltpu.VMEM((wide, (rows - 2) * cols), jnp.float32),
        ],
        compiler_params=PARAMS,
        cost_estimate=pl.CostEstimate(
            flops=2 * 9 * wide * depth * (rows - 2) * cols,
            bytes_accessed=2 * (kernel.size + x.size),
            transcendentals=0,
        ),
    )(x, kernel)


def weights_body(scale, starts_ref, field_ref, *refs):
    *grads, out_ref, shifted, total = refs
    shares, blocks, share, wide, cols = field_ref.shape
    rows, depth, _ = grads[0].shape
    height = blocks * rows
    edge = jnp.zeros((wide, cols), jnp.bfloat16)
    for tap in range(3):
        shifted[tap, :, 0:cols] = edge
        shifted[tap, :, (height + 1) * cols : (height + 2) * cols] = edge
    for place in range(rows):

        def shift_block(block, carry, place=place):
            piece = field_ref[place // share, block, place % share]
            span = pl.ds(pl.multiple_of((block * rows + place + 1) * cols, cols), cols)
            for tap in range(3):
                shifted[tap, :, span] = moved_columns(piece, tap - 1)
            return carry

        lax.fori_loop(0, blocks, shift_block, 0)
    for at, grad_ref in enumerate(grads):
        flat = jnp.concatenate([grad_ref[row] for row in range(rows)], axis=1)
        spans = [
            pl.ds(pl.multiple_of((starts_ref[at] + row_tap) * cols, cols), rows * cols)
            for row_tap in range(3)
        ]
        if wide % 16 == 0:
            windows = [shifted[:, :, span].reshape(3 * wide, rows * cols) for span in spans]
            product = lax.dot_general(
                jnp.concatenate(windows, axis=0),
                flat,
                (((1,), (1,)), ((), ())),
                preferred_element_type=jnp.float32,
            ).reshape(3, 3, wide, depth)
            total[...] = product if at == 0 else total[...] + product
        else:
            for row_tap in range(3):
                for tap in range(3):
                    product = lax.dot_general(
                        shifted[tap, :, spans[row_tap]],
                        flat,
                        (((1,), (1,)), ((), ())),
                        preferred_element_type=jnp.float32,
                    )
                    total[row_tap, tap] = product if at == 0 else total[row_tap, tap] + product
    out_ref[...] = total[...] * scale


def weight_grads(starts, field, grads):
    shares, blocks, share, wide, cols = field.shape
    rows, depth, _ = grads[0].shape
    height = blocks * rows
    out_shape = jax.ShapeDtypeStruct((3, 3, wide, depth), jnp.float32)
    vmem = pl.BlockSpec(memory_space=pltpu.VMEM)
    return pl.pallas_call(
        functools.partial(weights_body, 1.0 / height),
        in_specs=[pl.BlockSpec(memory_space=pltpu.SMEM), vmem, *[vmem for _ in grads]],
        out_specs=vmem,
        out_shape=out_shape,
        scratch_shapes=[
            pltpu.VMEM((3, wide, (height + 2) * cols), jnp.bfloat16),
            pltpu.VMEM(out_shape.shape, jnp.float32),
        ],
        compiler_params=PARAMS,
        cost_estimate=pl.CostEstimate(
            flops=2 * 9 * wide * depth * height * cols,
            bytes_accessed=2 * field.size + 2 * len(grads) * grads[0].size + 4 * 9 * wide * depth,
            transcendentals=0,
        ),
    )(starts, field, *grads)


def cycle_order(peers):
    return list(range(0, peers, 2)) + list(range(1, peers, 2))[::-1]


def ring_blocks(block, axis):
    peers = lax.axis_size(axis)
    order = cycle_order(peers)
    ahead = [(order[i], order[(i + 1) % peers]) for i in range(peers)]
    back = [(j, i) for i, j in ahead]
    blocks = [block]
    left = right = block
    for hop in range(1, peers // 2 + 1):
        left = lax.ppermute(left, axis, ahead)
        blocks.append(left)
        if hop <= (peers - 1) // 2:
            right = lax.ppermute(right, axis, back)
            blocks.append(right)
    return blocks


def ring_starts(axis, rows):
    peers = lax.axis_size(axis)
    order = cycle_order(peers)
    place = [order.index(i) for i in range(peers)]
    at = jnp.asarray(place, jnp.int32)[lax.axis_index(axis)]
    offsets = [0]
    for hop in range(1, peers // 2 + 1):
        offsets.append(-hop)
        if hop <= (peers - 1) // 2:
            offsets.append(hop)
    where = (at + jnp.asarray(offsets, jnp.int32)) % peers
    return jnp.asarray(order, jnp.int32)[where] * rows


def with_rims(shard, axis):
    peers = lax.axis_size(axis)
    up = [(i, i + 1) for i in range(peers - 1)]
    down = [(j, i) for i, j in up]
    before = lax.ppermute(shard[-1:], axis, up)
    after = lax.ppermute(shard[:1], axis, down)
    return jnp.concatenate([before, shard, after], axis=0)


def scatter_sum(blocks, axis, before=None):
    peers = lax.axis_size(axis)
    index = lax.axis_index(axis)
    own = lax.dynamic_index_in_dim(blocks, index, 0, keepdims=False)
    moved = []
    for step in range(1, peers):
        block = lax.dynamic_index_in_dim(blocks, (index + step) % peers, 0, keepdims=False)
        moved.append(lax.ppermute(block, axis, [(i, (i + step) % peers) for i in range(peers)]))
    own, before = lax.optimization_barrier((own, before))
    total = own.astype(jnp.float32)
    for block in moved:
        total = total + block.astype(jnp.float32)
    return total, before


def own_channels(field, axis, others):
    peers = lax.axis_size(axis)
    shares = lax.axis_size(others)
    rows, depth, cols = field.shape
    share = rows // shares
    part = lax.dynamic_slice_in_dim(field, lax.axis_index(others) * share, share, axis=0)
    part = part.reshape(share, peers, depth // peers, cols)
    part = jnp.transpose(part, (1, 0, 2, 3))
    part = lax.all_to_all(part, axis, 0, 0, tiled=True)
    return lax.all_gather(part, others, axis=0)


def on_device(
    latent,
    stale_latent,
    stale_hidden,
    first_kernel,
    second_kernel,
    scale_table,
    timestep,
    cotangent,
):
    row_index = lax.axis_index("rows")
    row_devices = lax.axis_size("rows")
    peers = lax.axis_size("chan")
    upright = lambda field: jnp.transpose(field, (0, 2, 1))
    latent, stale_latent, stale_hidden, cotangent = [
        upright(field) for field in (latent, stale_latent, stale_hidden, cotangent)
    ]
    first = jnp.transpose(first_kernel, (0, 1, 3, 2))
    second = jnp.transpose(second_kernel, (0, 1, 3, 2))
    rows, depth, cols = latent.shape
    latent_f = latent.astype(jnp.float32)
    act = jax.nn.silu(latent_f).astype(jnp.bfloat16)
    edge_act = jax.nn.silu(stale_latent.astype(jnp.float32)).astype(jnp.bfloat16)
    present = jnp.stack([row_index > 0, row_index < row_devices - 1])[:, None, None]
    edge_act = jnp.where(present, edge_act, jnp.zeros_like(edge_act))
    edge_hidden = jnp.where(present, stale_hidden, jnp.zeros_like(stale_hidden))
    act_pad = jnp.concatenate([edge_act[:1], act, edge_act[1:]], axis=0)
    act_all = lax.all_gather(act_pad, "chan", axis=1, tiled=True)
    step_scale = lax.dynamic_index_in_dim(scale_table, timestep[0], 0, keepdims=False)
    scale_map = jnp.broadcast_to(step_scale[:, None], (depth, cols))
    starts = ring_starts("rows", rows)

    cotangent_pad, ring_cotangent = lax.optimization_barrier(
        (with_rims(cotangent, "rows"), cotangent)
    )
    partial = backward_conv(cotangent_pad, second, peers)
    act_ready, partial = lax.optimization_barrier((act_all, partial))
    hidden_pad, slope = forward_conv(
        finish_hidden,
        act_ready,
        first,
        (edge_hidden, scale_map),
        [
            jax.ShapeDtypeStruct((rows + 2, depth, cols), jnp.bfloat16),
            jax.ShapeDtypeStruct((rows, depth, cols), jnp.float32),
        ],
    )
    grad_hidden, slope = scatter_sum(partial, "chan", slope)
    hidden_all = lax.all_gather(hidden_pad, "chan", axis=1, tiled=True)
    delta = (grad_hidden * slope).astype(jnp.bfloat16)
    delta_pad = with_rims(delta, "rows")
    delta_pad, ring_delta = lax.optimization_barrier((delta_pad, delta))
    partial = backward_conv(delta_pad, first, peers)
    hidden_ready, act_ready, partial = lax.optimization_barrier((hidden_all, act_ready, partial))
    hidden_own = own_channels(hidden_ready[1:-1], "rows", "chan")
    (output,) = forward_conv(
        finish_output,
        hidden_ready,
        second,
        (latent,),
        [jax.ShapeDtypeStruct((rows, depth, cols), jnp.bfloat16)],
    )
    grad_pre, output = scatter_sum(partial, "chan", output)
    grad_latent = (
        latent_f * 0.0 + cotangent.astype(jnp.float32) + grad_pre * silu_slope(latent_f)
    ).astype(jnp.bfloat16)
    act_own = own_channels(act_all[1:-1], "rows", "chan")
    grad_first = weight_grads(starts, act_own, ring_blocks(ring_delta, "rows"))
    grad_second = weight_grads(starts, hidden_own, ring_blocks(ring_cotangent, "rows"))
    return (upright(output), upright(grad_latent), grad_first, grad_second)


def solution(mesh):
    in_specs = (
        P("rows", None, "chan"),
        P("rows", None, "chan"),
        P("rows", None, "chan"),
        P(None, None, None, "chan"),
        P(None, None, None, "chan"),
        P(None, "chan"),
        P(),
        P("rows", None, "chan"),
    )
    out_specs = (
        P("rows", None, "chan"),
        P("rows", None, "chan"),
        P(None, None, "rows", "chan"),
        P(None, None, "rows", "chan"),
    )
    return jax.shard_map(
        on_device, mesh=mesh, in_specs=in_specs, out_specs=out_specs, check_vma=False
    )
```
